256 devices in a mesh: row: 32 (over z, x), col: 8 (over y, core).
Axes of the slice: x: 4, y: 4, z: 8, core: 2. Of those that a mesh axis runs over, the one named last changes fastest.
Arguments:
- panel_block: float32 [98304, 512], P('row', 'col'), may hold values from -1 to 1
- trailing: float32 [98304, 2048], P('row', 'col'), may hold values from -6 to 6
Outputs:
- triangle: float32 [512, 512], replicated
- coupling: float32 [512, 2048], P(None, 'col')
- updated: float32 [98304, 2048], P('row', 'col')
The draws below stay inside these ranges and needn't reach their ends.
All inputs are finite; a program needn't handle non-finite values.
Results may differ from the reference program's by a relative error of at most 0.0003.
Values sent between devices are 32-bit elements; how exact they have to be, the bound alone decides.
No kernel may reach another device: no remote copies, remote signals or barrier semaphores. Data moves between devices by JAX's collectives and lax.ppermute only.
A program may use at most 128 MiB of HBM per device.

```python
import jax
import jax.numpy as jnp
from jax import lax

B = 512
NC = 2048
ROWS = 98304


def draw_panel_block(key, part):
    first_key, second_key = jax.random.split(key)
    base = jax.random.normal(first_key, (ROWS, B), jnp.float32)
    mixing = jnp.eye(B, dtype=jnp.float32) + 0.6 * jax.random.normal(second_key, (B, B), jnp.float32) / B ** 0.5
    return jnp.dot(base, mixing, precision=lax.Precision.HIGHEST) * ROWS ** (-0.5)


def block_scale(rng, dims, pieces, low, top_value):
    gain = 1.0
    for position, shards_of in pieces:
        steps = jax.random.uniform(jax.random.fold_in(jax.random.fold_in(rng, 6), position), (shards_of,), jnp.float32, low / len(pieces), top_value / len(pieces))
        gain = gain * jnp.repeat(jnp.exp(steps), dims[position] // shards_of).reshape((-1,) + (1,) * (len(dims) - 1 - position))
    return gain


def bell_draw(own_key, dims, scale, reach, cuts=(), kind=jnp.bfloat16):
    factor_of = block_scale(own_key, dims, cuts, -0.22, 0.18) if cuts else 1.0
    result = jax.random.normal(own_key, dims, jnp.float32) * scale * factor_of
    return jnp.minimum(jnp.maximum(result, -reach), reach).astype(kind)


def setup_inputs(seed: int = 0) -> dict:
    seeds = jax.random.split(jax.random.key(seed), 3)
    return {
        "panel_block": draw_panel_block(jax.random.fold_in(seeds[2], 71), 0),
        "trailing": bell_draw(seeds[1], (ROWS, NC), 1.0, 6.0, ((0, 32), (1, 8)), jnp.float32),
    }


def reference(panel_block, trailing):
    orthonormal, triangle = jnp.linalg.qr(panel_block)
    sign_fix = jnp.where(jnp.diagonal(triangle) < 0, -1.0, 1.0).astype(jnp.float32)
    triangle = triangle * sign_fix[:, None]
    orthonormal = orthonormal * sign_fix[None, :]
    coupling = jnp.dot(orthonormal.T.astype(jnp.float32), trailing.astype(jnp.float32), precision=lax.Precision.HIGHEST, preferred_element_type=jnp.float32)
    updated = trailing - jnp.dot(orthonormal.astype(jnp.float32), coupling.astype(jnp.float32), precision=lax.Precision.HIGHEST, preferred_element_type=jnp.float32)
    return (triangle, coupling, updated)
```

```python
import jax
import jax.numpy as jnp
from jax import lax
from jax.experimental import pallas as pl
from jax.experimental.pallas import tpu as pltpu
from jax.sharding import Mesh
from jax.sharding import PartitionSpec as P

highest = lax.Precision.HIGHEST
LEAF = 64
LANES = 128

def spread(v, shape):
    return jnp.broadcast_to(v, shape)

def leaf_factor(block):
    groups = LEAF // 8
    full = (8, LANES)
    sub = lax.broadcasted_iota(jnp.int32, full, 0)
    x = [block[8 * i : 8 * i + 8] for i in range(groups)]
    done = []
    for kb in range(groups):
        cols = [
            [spread(x[i][:, 8 * kb + j : 8 * kb + j + 1], full) for i in range(kb, groups)]
            for j in range(8)
        ]
        pivots = jnp.ones(full, jnp.float32)
        for j in range(8):
            pivot = spread(cols[j][0][j : j + 1], full)
            pivots = jnp.where(sub == j, pivot, pivots)
            inverse = 1.0 / pivot
            tail = [spread(cols[jj][0][j : j + 1], full) * inverse for jj in range(j + 1, 8)]
            row = spread(x[kb][j : j + 1], full) * inverse
            for i in range(kb, groups):
                mult = cols[j][i - kb]
                if i == kb:
                    mult = jnp.where(sub > j, mult, 0.0)
                for jj in range(j + 1, 8):
                    cols[jj][i - kb] = cols[jj][i - kb] - mult * tail[jj - j - 1]
                x[i] = x[i] - mult * row
        done.append(x[kb] * (1.0 / jnp.sqrt(pivots)))
    return jnp.concatenate(done, axis=0)

def factor_kernel(gram_ref, upper_ref, inverse_ref, work):
    size = gram_ref.shape[0]
    blocks = size // LEAF
    lane = lax.broadcasted_iota(jnp.int32, (LEAF, LANES), 1)
    sub = lax.broadcasted_iota(jnp.int32, (LEAF, LANES), 0)
    place = lax.broadcasted_iota(jnp.int32, (LEAF, size), 1)
    depth = lax.broadcasted_iota(jnp.int32, (LEAF, size), 0)
    work[...] = gram_ref[...]
    for b in range(blocks):
        lo, hi = LEAF * b, LEAF * b + LEAF
        tile = LANES * (b // 2)
        square = work[lo:hi, tile : tile + LANES]
        if b % 2:
            square = pltpu.roll(square, LEAF, 1)
        both = leaf_factor(
            jnp.where(lane < LEAF, square, jnp.where(lane == sub + LEAF, 1.0, 0.0))
        )
        other = pltpu.roll(both, LEAF, 1)
        inv = other[:, :LEAF]
        rows = jnp.dot(inv, work[lo:hi, :], precision=highest, preferred_element_type=jnp.float32)
        inv_wide = jnp.concatenate([both if b % 2 else other] * (size // LANES), axis=1)
        own = (place >= lo) & (place < hi)
        upper_ref[lo:hi, :] = jnp.where(place >= lo + depth, rows, 0.0)
        rows_inv = jnp.where(own, inv_wide, rows)
        inverse_ref[lo:hi, :] = jnp.where(place <= lo + depth, rows_inv, 0.0)
        if b + 1 < blocks:
            mult = rows[:, hi - hi % LANES :]
            if hi % LANES:
                mult = mult[:, LEAF:]
            step = lax.dot_general(
                mult, rows_inv, (((0,), (0,)), ((), ())),
                precision=highest, preferred_element_type=jnp.float32,
            )
            below = lax.broadcasted_iota(jnp.int32, (size - hi, size), 1)
            kept = jnp.where((below >= lo) & (below < hi), 0.0, work[hi:, :])
            work[hi:, :] = kept - step

def factor(gram):
    size = gram.shape[0]
    return pl.pallas_call(
        factor_kernel,
        out_shape=[jax.ShapeDtypeStruct((size, size), jnp.float32)] * 2,
        in_specs=[pl.BlockSpec(memory_space=pltpu.VMEM)],
        out_specs=[pl.BlockSpec(memory_space=pltpu.VMEM)] * 2,
        scratch_shapes=[pltpu.VMEM((size, size), jnp.float32)],
        compiler_params=pltpu.CompilerParams(vmem_limit_bytes=32 * 2**20),
        name="factor",
    )(gram)


def dot(left, right, left_dim, right_dim, precision):
    return lax.dot_general(
        left, right, (((left_dim,), (right_dim,)), ((), ())),
        precision=precision, preferred_element_type=jnp.float32,
    )


def sum_over_rows(pieces, peers):
    arrived = lax.all_to_all(pieces, "row", 0, 0)
    summed = jnp.sum(arrived, axis=0)
    return lax.all_to_all(jnp.broadcast_to(summed, pieces.shape), "row", 0, 0)


def on_device(panel_block, trailing, peers):
    own = panel_block.T
    width = own.shape[0]
    gathered = lax.all_gather(own, "col", axis=0, tiled=True)
    size = gathered.shape[0]
    cols = trailing.shape[1]
    projected = dot(gathered, trailing, 1, 0, lax.Precision.HIGH)
    gram = dot(own, gathered, 1, 1, lax.Precision.HIGH)
    tiles_p = projected.reshape(peers, size // peers, cols // 128, 128).transpose(0, 2, 1, 3)
    tiles_p = tiles_p.reshape(peers, -1, 128)
    tiles_g = gram.reshape(width // 8, 8, size // 128, 128).transpose(0, 2, 1, 3)
    tiles_g = tiles_g.reshape(peers, -1, 128)
    both = sum_over_rows(jnp.concatenate([tiles_p, tiles_g], axis=1), peers)
    rows_p = size // peers * (cols // 128)
    tiles_p, tiles_g = both[:, :rows_p], both[:, rows_p:]
    projected = tiles_p.reshape(peers, cols // 128, size // peers, 128).transpose(0, 2, 1, 3)
    projected = projected.reshape(size, cols)
    gram = tiles_g.reshape(width // 8, size // 128, 8, 128).transpose(0, 2, 1, 3)
    gram = gram.reshape(width, size)
    gram = lax.all_to_all(jnp.broadcast_to(gram, (size // width, width, size)), "col", 0, 0)
    upper, inverse = factor(gram.reshape(size, size))
    coupling = dot(inverse, projected, 1, 0, highest)
    weights = dot(inverse, coupling, 0, 0, highest)
    updated = trailing - dot(gathered, weights, 0, 0, lax.Precision.HIGH)
    return (upper, coupling, updated)


def solution(mesh):
    placed = (P("row", "col"), P("row", "col"))
    peers = mesh.shape["row"]
    return jax.shard_map(
        lambda panel_block, trailing: on_device(panel_block, trailing, peers),
        mesh=mesh,
        in_specs=placed,
        out_specs=(P(), P(None, "col"), P("row", "col")),
        check_vma=False,
    )
```

```python
import jax
import jax.numpy as jnp
from jax import lax
from jax.experimental import pallas as pl
from jax.experimental.pallas import tpu as pltpu
from jax.sharding import Mesh
from jax.sharding import PartitionSpec as P

LEAF = 64
LANES = 128

def spread(v, shape):
    return jnp.broadcast_to(v, shape)

def leaf_factor(block):
    groups = LEAF // 8
    full = (8, LANES)
    sub = lax.broadcasted_iota(jnp.int32, full, 0)
    x = [block[8 * i : 8 * i + 8] for i in range(groups)]
    done = []
    for kb in range(groups):
        cols = [
            [spread(x[i][:, 8 * kb + j : 8 * kb + j + 1], full) for i in range(kb, groups)]
            for j in range(8)
        ]
        pivots = jnp.ones(full, jnp.float32)
        for j in range(8):
            pivot = spread(cols[j][0][j : j + 1], full)
            pivots = jnp.where(sub == j, pivot, pivots)
            inverse = 1.0 / pivot
            tail = [spread(cols[jj][0][j : j + 1], full) * inverse for jj in range(j + 1, 8)]
            row = spread(x[kb][j : j + 1], full) * inverse
            for i in range(kb, groups):
                mult = cols[j][i - kb]
                if i == kb:
                    mult = jnp.where(sub > j, mult, 0.0)
                for jj in range(j + 1, 8):
                    cols[jj][i - kb] = cols[jj][i - kb] - mult * tail[jj - j - 1]
                x[i] = x[i] - mult * row
        done.append(x[kb] * (1.0 / jnp.sqrt(pivots)))
    return jnp.concatenate(done, axis=0)

def thirds(value):
    first = value.astype(jnp.bfloat16)
    rest = value - first.astype(jnp.float32)
    second = rest.astype(jnp.bfloat16)
    return first, second, (rest - second.astype(jnp.float32)).astype(jnp.bfloat16)


def six_left(value, axis):
    one, two, three = thirds(value)
    return jnp.concatenate([one, one, two, one, two, three], axis=axis)


def six_right(value):
    one, two, three = thirds(value)
    return jnp.concatenate([one, two, one, three, two, one], axis=0)


def factor_kernel(place_ref, mine_ref, other_ref, upper_ref, inverse_ref, work):
    size = work.shape[0]
    blocks = size // LEAF
    lane = lax.broadcasted_iota(jnp.int32, (LEAF, LANES), 1)
    sub = lax.broadcasted_iota(jnp.int32, (LEAF, LANES), 0)
    place = lax.broadcasted_iota(jnp.int32, (LEAF, size), 1)
    depth = lax.broadcasted_iota(jnp.int32, (LEAF, size), 0)
    y, core = place_ref[0], place_ref[1]
    for dy in range(4):
        owner = lax.rem(y + dy, 4)
        for ref, side in ((mine_ref, core), (other_ref, 1 - core)):
            for tile in range(ref.shape[1]):
                to = pl.multiple_of(128 * owner + 64 * side + 8 * (tile // 4), 8)
                lanes = pl.multiple_of(128 * lax.rem(owner + tile % 4, 4), 128)
                work[pl.ds(to, 8), pl.ds(lanes, 128)] = ref[dy, tile]
    for b in range(blocks):
        lo, hi = LEAF * b, LEAF * b + LEAF
        tile = LANES * (b // 2)
        square = work[lo:hi, tile : tile + LANES]
        if b % 2:
            square = pltpu.roll(square, LEAF, 1)
        both = leaf_factor(
            jnp.where(lane < LEAF, square, jnp.where(lane == sub + LEAF, 1.0, 0.0))
        )
        other = pltpu.roll(both, LEAF, 1)
        inv = other[:, :LEAF]
        rows = jnp.dot(
            six_left(inv, 1), six_right(work[lo:hi, :]), preferred_element_type=jnp.float32
        )
        inv_wide = jnp.concatenate([both if b % 2 else other] * (size // LANES), axis=1)
        own = (place >= lo) & (place < hi)
        upper_ref[lo:hi, :] = jnp.where(place >= lo + depth, rows, 0.0)
        rows_inv = jnp.where(own, inv_wide, rows)
        inverse_ref[lo:hi, :] = jnp.where(place <= lo + depth, rows_inv, 0.0)
        if b + 1 < blocks:
            mult = rows[:, hi - hi % LANES :]
            if hi % LANES:
                mult = mult[:, LEAF:]
            step = lax.dot_general(
                six_left(mult, 0), six_right(rows_inv), (((0,), (0,)), ((), ())),
                preferred_element_type=jnp.float32,
            )
            below = lax.broadcasted_iota(jnp.int32, (size - hi, size), 1)
            kept = jnp.where((below >= lo) & (below < hi), 0.0, work[hi:, :])
            work[hi:, :] = kept - step

def factor(place, mine, other):
    size = 512
    return pl.pallas_call(
        factor_kernel,
        out_shape=[jax.ShapeDtypeStruct((size, size), jnp.float32)] * 2,
        in_specs=[
            pl.BlockSpec(memory_space=pltpu.SMEM),
            pl.BlockSpec(memory_space=pltpu.VMEM),
            pl.BlockSpec(memory_space=pltpu.VMEM),
        ],
        out_specs=[pl.BlockSpec(memory_space=pltpu.VMEM)] * 2,
        scratch_shapes=[pltpu.VMEM((size, size), jnp.float32)],
        compiler_params=pltpu.CompilerParams(vmem_limit_bytes=56 * 2**20),
        cost_estimate=pl.CostEstimate(
            flops=25 * 10**9, bytes_accessed=4 * 10**6, transcendentals=0
        ),
        name="factor",
    )(place, mine, other)


STEPS = 3


def halves(value):
    high = value.astype(jnp.bfloat16)
    return high, (value - high.astype(jnp.float32)).astype(jnp.bfloat16)


def product(a, b):
    return lax.dot_general(a, b, (((1,), (0,)), ((), ())), preferred_element_type=jnp.float32)


def dot3(both, high, right):
    rows = high.shape[0]
    right_high, right_low = halves(right)
    first = product(both, right_high)
    return first[:rows] + (first[rows:] + product(high, right_low))


def dot4(both, right):
    rows, cols = both.shape[0] // 2, right.shape[1]
    four = product(both, jnp.concatenate(halves(right), axis=1))
    return four[:rows, :cols] + (four[rows:, :cols] + four[:rows, cols:] + four[rows:, cols:])


def dot6(left, right):
    rows = left.shape[0]
    left, right = thirds(left), thirds(right)
    first = product(jnp.concatenate(left, axis=0), right[0])
    second = product(jnp.concatenate(left[:2], axis=0), right[1])
    small = first[2 * rows :] + (second[rows:] + product(left[0], right[2]))
    return first[:rows] + (first[rows : 2 * rows] + second[:rows] + small)


def chunk(k, length):
    return pl.ds(pl.multiple_of(k * length, 128), length)


def fetches(k, depth, trailing_ref, trailing_buf, block_refs, block_buf, sems, starts=None):
    part = chunk(k, depth)
    copies = [pltpu.make_async_copy(trailing_ref.at[part], trailing_buf.at[part], sems.at[k, 0])]
    at = 0
    for index, ref in enumerate(block_refs):
        rows = ref.shape[0]
        to = pl.ds(at if starts is None else pl.multiple_of(starts[index], 32), rows)
        copies.append(
            pltpu.make_async_copy(ref.at[:, part], block_buf.at[to, part], sems.at[k, index + 1])
        )
        at += rows
    return copies


def start_all(*places):
    for k in range(STEPS):
        for copy in fetches(k, *places):
            copy.start()


def wait_chunk(k, *places):
    for copy in fetches(k, *places):
        copy.wait()


def accumulate(places, rows, proj_ref, gram_ref):
    depth, _, trailing_buf, _, block_buf, _ = places
    own_at = rows if block_buf.shape[0] > rows else 0
    start_all(*places)
    proj_ref[...] = jnp.zeros_like(proj_ref)
    gram_ref[...] = jnp.zeros_like(gram_ref)

    @pl.loop(0, STEPS)
    def _(k):
        wait_chunk(k, *places)
        part = chunk(k, depth)
        high, low = halves(block_buf[:rows, part])
        both = jnp.concatenate([high, low], axis=0)
        proj_ref[...] += dot3(both, high, trailing_buf[part])
        gram_ref[...] += dot4(both, block_buf[own_at : own_at + 64, part].T)


def first_kernel(trailing_ref, *refs):
    *block_refs, proj_ref, gram_ref, trailing_buf, block_buf, sems = refs
    depth = trailing_ref.shape[0] // STEPS
    places = (depth, trailing_ref, trailing_buf, block_refs, block_buf, sems)
    accumulate(places, block_buf.shape[0], proj_ref, gram_ref)


def last_kernel(core_ref, trailing_ref, *refs):
    *block_refs, proj_early, gram_early, proj_out, gram_out = refs[:-5]
    trailing_buf, block_buf, sems, proj_ref, gram_ref = refs[-5:]
    depth = trailing_ref.shape[0] // STEPS
    places = (depth, trailing_ref, trailing_buf, block_refs, block_buf, sems)
    accumulate(places, proj_ref.shape[0], proj_ref, gram_ref)

    def ordered(early, late):
        return [early[0:128], early[128:256], late, early[256:384]]

    peers, per = proj_out.shape[0], proj_out.shape[1] // 2
    proj = jnp.concatenate(ordered(proj_early[...], proj_ref[...]), axis=0)
    for side in range(2):
        part = proj[:, 128 * side : 128 * side + 128]
        proj_out[:, per * side : per * side + per, :] = part.reshape(peers, per, 128)
    for place, pair in enumerate(ordered(gram_early[...], gram_ref[...])):
        tile = pair.T
        tile = jnp.where(core_ref[0] == 1, pltpu.roll(tile, 64, 1), tile)
        for group in range(tile.shape[0] // 8):
            gram_out[4 * group + place] = tile[8 * group : 8 * group + 8]


def whole_spec(shape):
    return pl.BlockSpec(memory_space=pltpu.VMEM)


def in_place():
    return pl.BlockSpec(memory_space=pl.ANY)


def float_shape(*shape):
    return jax.ShapeDtypeStruct(shape, jnp.float32)


def buffers(trailing, rows, blocks):
    return [
        pltpu.VMEM(trailing.shape, jnp.float32),
        pltpu.VMEM((rows, trailing.shape[0]), jnp.float32),
        pltpu.SemaphoreType.DMA((STEPS, 1 + len(blocks))),
    ]


def project_first(trailing, blocks):
    rows = sum(block.shape[0] for block in blocks)
    shapes = [(rows, trailing.shape[1]), (rows, 64)]
    return pl.pallas_call(
        first_kernel,
        out_shape=[float_shape(*shape) for shape in shapes],
        in_specs=[in_place()] * (1 + len(blocks)),
        out_specs=[whole_spec(shape) for shape in shapes],
        scratch_shapes=buffers(trailing, rows, blocks),
        compiler_params=pltpu.CompilerParams(vmem_limit_bytes=56 * 2**20),
        cost_estimate=pl.CostEstimate(
            flops=15 * 10**9, bytes_accessed=6 * 10**6, transcendentals=0
        ),
        name="project_first",
    )(trailing, *blocks)


def project_last(core, trailing, own, blocks, proj_early, gram_early, peers):
    rows = sum(block.shape[0] for block in blocks)
    size = rows + proj_early.shape[0]
    per = size // peers * (trailing.shape[1] // 128)
    shapes = [(peers, per, 128), (4 * own.shape[0] // 8, 8, 128)]
    return pl.pallas_call(
        last_kernel,
        out_shape=[float_shape(*shape) for shape in shapes],
        in_specs=[
            pl.BlockSpec(memory_space=pltpu.SMEM),
            *[in_place()] * (2 + len(blocks)),
            whole_spec(proj_early.shape),
            whole_spec(gram_early.shape),
        ],
        out_specs=[whole_spec(shape) for shape in shapes],
        scratch_shapes=[
            *buffers(trailing, rows + own.shape[0], [*blocks, own]),
            pltpu.VMEM((rows, trailing.shape[1]), jnp.float32),
            pltpu.VMEM((rows, own.shape[0]), jnp.float32),
        ],
        compiler_params=pltpu.CompilerParams(vmem_limit_bytes=56 * 2**20),
        cost_estimate=pl.CostEstimate(flops=10**9, bytes_accessed=6 * 10**6, transcendentals=0),
        name="project_last",
    )(core, trailing, *blocks, own, proj_early, gram_early)


def update_kernel(place_ref, proj_ref, inverse_ref, trailing_ref, *refs):
    *block_refs, coupling_ref, updated_ref = refs[:-6]
    trailing_buf, block_buf, sems, both_ref, hold_ref, out_sems = refs[-6:]
    depth = trailing_ref.shape[0] // STEPS
    cols = coupling_ref.shape[1]
    size = inverse_ref.shape[0]
    y, core = place_ref[0], place_ref[1]

    def column(dy, other):
        return 128 * lax.rem(y + dy, 4) + 64 * lax.rem(core + other, 2)

    starts = [column(0, 0), column(0, 1)]
    for dy in range(1, 4):
        for other in range(2):
            starts += [column(dy, other), column(dy, other) + 32]
    places = (depth, trailing_ref, trailing_buf, block_refs, block_buf, sems, starts)
    start_all(*places)
    peers, per = proj_ref.shape[0], proj_ref.shape[1] // 2
    sides = [proj_ref[:, per * s : per * s + per, :].reshape(size, 128) for s in range(2)]
    proj = jnp.concatenate(sides, axis=1)
    for dy in range(4):
        for other in range(2):
            slot = 64 * (2 * dy + other)
            to = pl.multiple_of(column(dy, other), 64)
            hold_ref[pl.ds(to, 64), :] = proj[slot : slot + 64]
    inverse = inverse_ref[...]
    coupling = dot6(inverse, hold_ref[...])
    coupling_ref[...] = coupling
    both_ref[:cols], both_ref[cols:] = halves(dot6(coupling.T, inverse))

    def send(k):
        part = chunk(k, depth)
        return pltpu.make_async_copy(trailing_buf.at[part], updated_ref.at[part], out_sems.at[k])

    @pl.loop(0, STEPS)
    def _(k):
        wait_chunk(k, *places)
        part = chunk(k, depth)
        change = dot3(both_ref[...], both_ref[:cols, :], block_buf[:, part])
        trailing_buf[part] = trailing_buf[part] - change.T
        send(k).start()

    for k in range(STEPS):
        send(k).wait()


def update(place, projected, inverse, trailing, blocks):
    size, cols = inverse.shape[0], trailing.shape[1]
    return pl.pallas_call(
        update_kernel,
        out_shape=[float_shape(size, cols), float_shape(*trailing.shape)],
        in_specs=[
            pl.BlockSpec(memory_space=pltpu.SMEM),
            whole_spec(projected.shape),
            whole_spec(inverse.shape),
            *[in_place()] * (1 + len(blocks)),
        ],
        out_specs=[whole_spec((size, cols)), in_place()],
        scratch_shapes=[
            *buffers(trailing, size, blocks),
            pltpu.VMEM((2 * cols, size), jnp.bfloat16),
            pltpu.VMEM((size, cols), jnp.float32),
            pltpu.SemaphoreType.DMA((STEPS,)),
        ],
        compiler_params=pltpu.CompilerParams(vmem_limit_bytes=56 * 2**20),
        cost_estimate=pl.CostEstimate(
            flops=3 * 10**9, bytes_accessed=13 * 10**6, transcendentals=0
        ),
        name="update",
    )(place, projected, inverse, trailing, *blocks)


def shift(value, axis, length, step):
    return lax.ppermute(value, axis, [(i, (i + step) % length) for i in range(length)])


def swap(value):
    return shift(value, "core", 2, 1)


def sum_over_rows(pieces):
    summed = jnp.sum(lax.all_to_all(pieces, ("z", "x"), 0, 0), axis=0)
    return lax.all_to_all(jnp.broadcast_to(summed, pieces.shape), ("z", "x"), 0, 0)


def on_device(panel_block, trailing):
    peers = lax.axis_size(("z", "x"))
    y, core = lax.axis_index("y"), lax.axis_index("core")
    own = panel_block.T
    low, high = own[:32], own[32:]
    below = [shift(low, "y", 4, 1), shift(high, "y", 4, 1)]
    above = [shift(low, "y", 4, -1), shift(high, "y", 4, -1)]
    far = [shift(below[0], "y", 4, 1), shift(above[1], "y", 4, -1)]
    own_other = swap(own)
    below_other, above_other = ([swap(v) for v in vs] for vs in (below, above))
    near = [own, own_other, *above, *above_other, *below, *below_other]
    early, far_now = lax.optimization_barrier((project_first(trailing, near), far))
    far_other = [swap(v) for v in far_now]
    proj, gram = project_last(core[None], trailing, own, [*far, *far_other], *early, peers)
    gram = sum_over_rows(gram)
    gram, proj = lax.optimization_barrier((gram, proj))
    grams = jnp.stack([gram, *(shift(gram, "y", 4, -dy) for dy in range(1, 4))])
    proj = sum_over_rows(proj)
    upper, inverse = factor(jnp.stack([y, core]), grams, swap(grams))
    blocks = [own, own_other, *above, *above_other, *far, *far_other, *below, *below_other]
    coupling, updated = update(jnp.stack([y, core]), proj, inverse, trailing, blocks)
    return (upper, coupling, updated)


def solution(mesh):
    physical = Mesh(mesh.devices.reshape(8, 4, 4, 2), ("z", "x", "y", "core"))
    row, col = ("z", "x"), ("y", "core")
    return jax.shard_map(
        on_device,
        mesh=physical,
        in_specs=(P(row, col), P(row, col)),
        out_specs=(P(), P(None, col), P(row, col)),
        check_vma=False,
    )
```

```python
import functools

import jax
import jax.numpy as jnp
from jax import lax
from jax.experimental import pallas as pl
from jax.experimental.pallas import tpu as pltpu
from jax.sharding import Mesh
from jax.sharding import PartitionSpec as P

LEAF = 64
LANES = 128

def spread(v, shape):
    return jnp.broadcast_to(v, shape)

def leaf_factor(block):
    groups = LEAF // 8
    full = (8, LANES)
    sub = lax.broadcasted_iota(jnp.int32, full, 0)
    x = [block[8 * i : 8 * i + 8] for i in range(groups)]
    done = []
    for kb in range(groups):
        cols = [
            [spread(x[i][:, 8 * kb + j : 8 * kb + j + 1], full) for i in range(kb, groups)]
            for j in range(8)
        ]
        pivots = jnp.ones(full, jnp.float32)
        for j in range(8):
            pivot = spread(cols[j][0][j : j + 1], full)
            pivots = jnp.where(sub == j, pivot, pivots)
            inverse = 1.0 / pivot
            tail = [spread(cols[jj][0][j : j + 1], full) * inverse for jj in range(j + 1, 8)]
            row = spread(x[kb][j : j + 1], full) * inverse
            for i in range(kb, groups):
                mult = cols[j][i - kb]
                if i == kb:
                    mult = jnp.where(sub > j, mult, 0.0)
                for jj in range(j + 1, 8):
                    cols[jj][i - kb] = cols[jj][i - kb] - mult * tail[jj - j - 1]
                x[i] = x[i] - mult * row
        done.append(x[kb] * (1.0 / jnp.sqrt(pivots)))
    return jnp.concatenate(done, axis=0)

def thirds(value):
    first = value.astype(jnp.bfloat16)
    rest = value - first.astype(jnp.float32)
    second = rest.astype(jnp.bfloat16)
    return first, second, (rest - second.astype(jnp.float32)).astype(jnp.bfloat16)


def six_left(value, axis):
    one, two, three = thirds(value)
    return jnp.concatenate([one, one, two, one, two, three], axis=axis)


def six_right(value):
    one, two, three = thirds(value)
    return jnp.concatenate([one, two, one, three, two, one], axis=0)


def factor_kernel(place_ref, mine_ref, other_ref, upper_ref, inverse_ref, work):
    size = work.shape[0]
    blocks = size // LEAF
    lane = lax.broadcasted_iota(jnp.int32, (LEAF, LANES), 1)
    sub = lax.broadcasted_iota(jnp.int32, (LEAF, LANES), 0)
    place = lax.broadcasted_iota(jnp.int32, (LEAF, size), 1)
    depth = lax.broadcasted_iota(jnp.int32, (LEAF, size), 0)
    y, core = place_ref[0], place_ref[1]
    for dy in range(4):
        owner = lax.rem(y + dy, 4)
        for ref, side in ((mine_ref, core), (other_ref, 1 - core)):
            for tile in range(ref.shape[1]):
                to = pl.multiple_of(128 * owner + 64 * side + 8 * (tile // 4), 8)
                lanes = pl.multiple_of(128 * lax.rem(owner + tile % 4, 4), 128)
                work[pl.ds(to, 8), pl.ds(lanes, 128)] = ref[dy, tile]
    late = None
    for b in range(blocks):
        lo, hi = LEAF * b, LEAF * b + LEAF
        tile = LANES * (b // 2)
        square = work[lo:hi, tile : tile + LANES]
        if b % 2:
            square = pltpu.roll(square, LEAF, 1)
        both = leaf_factor(
            jnp.where(lane < LEAF, square, jnp.where(lane == sub + LEAF, 1.0, 0.0))
        )
        other = pltpu.roll(both, LEAF, 1)
        inv = other[:, :LEAF]
        rows = jnp.dot(
            six_left(inv, 1), six_right(work[lo:hi, :]), preferred_element_type=jnp.float32
        )
        inv_wide = jnp.concatenate([both if b % 2 else other] * (size // LANES), axis=1)
        own = (place >= lo) & (place < hi)
        upper_ref[lo:hi, :] = jnp.where(place >= lo + depth, rows, 0.0)
        rows_inv = jnp.where(own, inv_wide, rows)
        inverse_ref[lo:hi, :] = jnp.where(place <= lo + depth, rows_inv, 0.0)
        if late is not None:
            late()
            late = None
        if b + 1 < blocks:
            mult = rows[:, hi - hi % LANES :]
            if hi % LANES:
                mult = mult[:, LEAF:]
            left, right = six_left(mult, 0), six_right(rows_inv)
            cut = min(hi + LEAF, size)

            def subtract(start, stop, lo=lo, hi=hi, left=left, right=right):
                step = lax.dot_general(
                    left[:, start - hi : stop - hi], right, (((0,), (0,)), ((), ())),
                    preferred_element_type=jnp.float32,
                )
                lanes = lax.broadcasted_iota(jnp.int32, (stop - start, size), 1)
                kept = jnp.where((lanes >= lo) & (lanes < hi), 0.0, work[start:stop, :])
                work[start:stop, :] = kept - step

            subtract(hi, cut)
            if cut < size:
                late = functools.partial(subtract, cut, size)


def factor(place, mine, other):
    size = 512
    return pl.pallas_call(
        factor_kernel,
        out_shape=[jax.ShapeDtypeStruct((size, size), jnp.float32)] * 2,
        in_specs=[
            pl.BlockSpec(memory_space=pltpu.SMEM),
            pl.BlockSpec(memory_space=pltpu.VMEM),
            pl.BlockSpec(memory_space=pltpu.VMEM),
        ],
        out_specs=[pl.BlockSpec(memory_space=pltpu.VMEM)] * 2,
        scratch_shapes=[pltpu.VMEM((size, size), jnp.float32)],
        compiler_params=pltpu.CompilerParams(vmem_limit_bytes=56 * 2**20),
        cost_estimate=pl.CostEstimate(
            flops=25 * 10**9, bytes_accessed=4 * 10**6, transcendentals=0
        ),
        name="factor",
    )(place, mine, other)


STEPS = 3


def halves(value):
    high = value.astype(jnp.bfloat16)
    return high, (value - high.astype(jnp.float32)).astype(jnp.bfloat16)


def product(a, b):
    return lax.dot_general(a, b, (((1,), (0,)), ((), ())), preferred_element_type=jnp.float32)


def dot3(both, high, right):
    rows = high.shape[0]
    right_high, right_low = halves(right)
    first = product(both, right_high)
    return first[:rows] + (first[rows:] + product(high, right_low))


def dot4(both, right):
    rows, cols = both.shape[0] // 2, right.shape[1]
    four = product(both, jnp.concatenate(halves(right), axis=1))
    return four[:rows, :cols] + (four[rows:, :cols] + four[:rows, cols:] + four[rows:, cols:])


def dot6(left, right):
    rows = left.shape[0]
    left, right = thirds(left), thirds(right)
    first = product(jnp.concatenate(left, axis=0), right[0])
    second = product(jnp.concatenate(left[:2], axis=0), right[1])
    small = first[2 * rows :] + (second[rows:] + product(left[0], right[2]))
    return first[:rows] + (first[rows : 2 * rows] + second[:rows] + small)


def chunk(k, length):
    return pl.ds(pl.multiple_of(k * length, 128), length)


def fetches(k, depth, trailing_ref, trailing_buf, block_refs, block_buf, sems, starts=None):
    part = chunk(k, depth)
    copies = [pltpu.make_async_copy(trailing_ref.at[part], trailing_buf.at[part], sems.at[k, 0])]
    at = 0
    for index, ref in enumerate(block_refs):
        rows = ref.shape[0]
        to = pl.ds(at if starts is None else pl.multiple_of(starts[index], 32), rows)
        copies.append(
            pltpu.make_async_copy(ref.at[:, part], block_buf.at[to, part], sems.at[k, index + 1])
        )
        at += rows
    return copies


def start_all(*places):
    for k in range(STEPS):
        for copy in fetches(k, *places):
            copy.start()


def wait_chunk(k, *places):
    for copy in fetches(k, *places):
        copy.wait()


def accumulate(places, rows, proj_ref, gram_ref):
    depth, _, trailing_buf, _, block_buf, _ = places
    own_at = rows if block_buf.shape[0] > rows else 0
    start_all(*places)
    proj_ref[...] = jnp.zeros_like(proj_ref)
    gram_ref[...] = jnp.zeros_like(gram_ref)

    @pl.loop(0, STEPS)
    def _(k):
        wait_chunk(k, *places)
        part = chunk(k, depth)
        high, low = halves(block_buf[:rows, part])
        both = jnp.concatenate([high, low], axis=0)
        proj_ref[...] += dot3(both, high, trailing_buf[part])
        gram_ref[...] += dot4(both, block_buf[own_at : own_at + 64, part].T)


def first_kernel(trailing_ref, *refs):
    *block_refs, proj_ref, gram_ref, trailing_buf, block_buf, sems = refs
    depth = trailing_ref.shape[0] // STEPS
    places = (depth, trailing_ref, trailing_buf, block_refs, block_buf, sems)
    accumulate(places, block_buf.shape[0], proj_ref, gram_ref)


def last_kernel(core_ref, trailing_ref, *refs):
    *block_refs, proj_early, gram_early, proj_out, gram_out = refs[:-5]
    trailing_buf, block_buf, sems, proj_ref, gram_ref = refs[-5:]
    depth = trailing_ref.shape[0] // STEPS
    places = (depth, trailing_ref, trailing_buf, block_refs, block_buf, sems)
    accumulate(places, proj_ref.shape[0], proj_ref, gram_ref)

    def ordered(early, late):
        return [early[0:128], early[128:256], late, early[256:384]]

    peers, per = proj_out.shape[0], proj_out.shape[1] // 2
    proj = jnp.concatenate(ordered(proj_early[...], proj_ref[...]), axis=0)
    for side in range(2):
        part = proj[:, 128 * side : 128 * side + 128]
        proj_out[:, per * side : per * side + per, :] = part.reshape(peers, per, 128)
    for place, pair in enumerate(ordered(gram_early[...], gram_ref[...])):
        tile = pair.T
        tile = jnp.where(core_ref[0] == 1, pltpu.roll(tile, 64, 1), tile)
        for group in range(tile.shape[0] // 8):
            gram_out[4 * group + place] = tile[8 * group : 8 * group + 8]


def whole_spec(shape):
    return pl.BlockSpec(memory_space=pltpu.VMEM)


def in_place():
    return pl.BlockSpec(memory_space=pl.ANY)


def float_shape(*shape):
    return jax.ShapeDtypeStruct(shape, jnp.float32)


def buffers(trailing, rows, blocks):
    return [
        pltpu.VMEM(trailing.shape, jnp.float32),
        pltpu.VMEM((rows, trailing.shape[0]), jnp.float32),
        pltpu.SemaphoreType.DMA((STEPS, 1 + len(blocks))),
    ]


def project_first(trailing, blocks):
    rows = sum(block.shape[0] for block in blocks)
    shapes = [(rows, trailing.shape[1]), (rows, 64)]
    return pl.pallas_call(
        first_kernel,
        out_shape=[float_shape(*shape) for shape in shapes],
        in_specs=[in_place()] * (1 + len(blocks)),
        out_specs=[whole_spec(shape) for shape in shapes],
        scratch_shapes=buffers(trailing, rows, blocks),
        compiler_params=pltpu.CompilerParams(vmem_limit_bytes=56 * 2**20),
        cost_estimate=pl.CostEstimate(
            flops=15 * 10**9, bytes_accessed=6 * 10**6, transcendentals=0
        ),
        name="project_first",
    )(trailing, *blocks)


def project_last(core, trailing, own, blocks, proj_early, gram_early, peers):
    rows = sum(block.shape[0] for block in blocks)
    size = rows + proj_early.shape[0]
    per = size // peers * (trailing.shape[1] // 128)
    shapes = [(peers, per, 128), (4 * own.shape[0] // 8, 8, 128)]
    return pl.pallas_call(
        last_kernel,
        out_shape=[float_shape(*shape) for shape in shapes],
        in_specs=[
            pl.BlockSpec(memory_space=pltpu.SMEM),
            *[in_place()] * (2 + len(blocks)),
            whole_spec(proj_early.shape),
            whole_spec(gram_early.shape),
        ],
        out_specs=[whole_spec(shape) for shape in shapes],
        scratch_shapes=[
            *buffers(trailing, rows + own.shape[0], [*blocks, own]),
            pltpu.VMEM((rows, trailing.shape[1]), jnp.float32),
            pltpu.VMEM((rows, own.shape[0]), jnp.float32),
        ],
        compiler_params=pltpu.CompilerParams(vmem_limit_bytes=56 * 2**20),
        cost_estimate=pl.CostEstimate(flops=10**9, bytes_accessed=6 * 10**6, transcendentals=0),
        name="project_last",
    )(core, trailing, *blocks, own, proj_early, gram_early)


def update_kernel(place_ref, proj_ref, inverse_ref, trailing_ref, *refs):
    *block_refs, coupling_ref, updated_ref = refs[:-6]
    trailing_buf, block_buf, sems, both_ref, hold_ref, out_sems = refs[-6:]
    depth = trailing_ref.shape[0] // STEPS
    cols = coupling_ref.shape[1]
    size = inverse_ref.shape[0]
    y, core = place_ref[0], place_ref[1]

    def column(dy, other):
        return 128 * lax.rem(y + dy, 4) + 64 * lax.rem(core + other, 2)

    starts = [column(0, 0), column(0, 1)]
    for dy in range(1, 4):
        for other in range(2):
            starts += [column(dy, other), column(dy, other) + 32]
    places = (depth, trailing_ref, trailing_buf, block_refs, block_buf, sems, starts)
    start_all(*places)
    peers, per = proj_ref.shape[0], proj_ref.shape[1] // 2
    sides = [proj_ref[:, per * s : per * s + per, :].reshape(size, 128) for s in range(2)]
    proj = jnp.concatenate(sides, axis=1)
    for dy in range(4):
        for other in range(2):
            slot = 64 * (2 * dy + other)
            to = pl.multiple_of(column(dy, other), 64)
            hold_ref[pl.ds(to, 64), :] = proj[slot : slot + 64]
    inverse = inverse_ref[...]
    coupling = dot6(inverse, hold_ref[...])
    coupling_ref[...] = coupling
    both_ref[:cols], both_ref[cols:] = halves(dot6(coupling.T, inverse))

    def send(k):
        part = chunk(k, depth)
        return pltpu.make_async_copy(trailing_buf.at[part], updated_ref.at[part], out_sems.at[k])

    @pl.loop(0, STEPS)
    def _(k):
        wait_chunk(k, *places)
        part = chunk(k, depth)
        change = dot3(both_ref[...], both_ref[:cols, :], block_buf[:, part])
        trailing_buf[part] = trailing_buf[part] - change.T
        send(k).start()

    for k in range(STEPS):
        send(k).wait()


def update(place, projected, inverse, trailing, blocks):
    size, cols = inverse.shape[0], trailing.shape[1]
    return pl.pallas_call(
        update_kernel,
        out_shape=[float_shape(size, cols), float_shape(*trailing.shape)],
        in_specs=[
            pl.BlockSpec(memory_space=pltpu.SMEM),
            whole_spec(projected.shape),
            whole_spec(inverse.shape),
            *[in_place()] * (1 + len(blocks)),
        ],
        out_specs=[whole_spec((size, cols)), in_place()],
        scratch_shapes=[
            *buffers(trailing, size, blocks),
            pltpu.VMEM((2 * cols, size), jnp.bfloat16),
            pltpu.VMEM((size, cols), jnp.float32),
            pltpu.SemaphoreType.DMA((STEPS,)),
        ],
        compiler_params=pltpu.CompilerParams(vmem_limit_bytes=56 * 2**20),
        cost_estimate=pl.CostEstimate(
            flops=3 * 10**9, bytes_accessed=13 * 10**6, transcendentals=0
        ),
        name="update",
    )(place, projected, inverse, trailing, *blocks)


def shift(value, axis, length, step):
    return lax.ppermute(value, axis, [(i, (i + step) % length) for i in range(length)])


def swap(value):
    return shift(value, "core", 2, 1)


def sum_over_rows(pieces):
    summed = jnp.sum(lax.all_to_all(pieces, ("z", "x"), 0, 0), axis=0)
    return lax.all_to_all(jnp.broadcast_to(summed, pieces.shape), ("z", "x"), 0, 0)


def on_device(panel_block, trailing):
    peers = lax.axis_size(("z", "x"))
    y, core = lax.axis_index("y"), lax.axis_index("core")
    own = panel_block.T
    low, high = own[:32], own[32:]
    own_other = swap(own)
    below_low, above_high = shift(low, "y", 4, 1), shift(high, "y", 4, -1)
    far = [shift(below_low, "y", 4, 1), shift(above_high, "y", 4, -1)]
    low, high, own_other = lax.optimization_barrier((low, high, own_other))
    below = [below_low, shift(high, "y", 4, 1)]
    above = [shift(low, "y", 4, -1), above_high]
    below_other, above_other = ([swap(v) for v in vs] for vs in (below, above))
    near = [own, own_other, *above, *above_other, *below, *below_other]
    early, far_now = lax.optimization_barrier((project_first(trailing, near), far))
    far_other = [swap(v) for v in far_now]
    proj, gram = project_last(core[None], trailing, own, [*far, *far_other], *early, peers)
    gram = sum_over_rows(gram)
    gram, proj = lax.optimization_barrier((gram, proj))
    grams = jnp.stack([gram, *(shift(gram, "y", 4, -dy) for dy in range(1, 4))])
    proj = sum_over_rows(proj)
    upper, inverse = factor(jnp.stack([y, core]), grams, swap(grams))
    blocks = [own, own_other, *above, *above_other, *far, *far_other, *below, *below_other]
    coupling, updated = update(jnp.stack([y, core]), proj, inverse, trailing, blocks)
    return (upper, coupling, updated)


def solution(mesh):
    physical = Mesh(mesh.devices.reshape(8, 4, 4, 2), ("z", "x", "y", "core"))
    row, col = ("z", "x"), ("y", "core")
    return jax.shard_map(
        on_device,
        mesh=physical,
        in_specs=(P(row, col), P(row, col)),
        out_specs=(P(), P(None, col), P(row, col)),
        check_vma=False,
    )
```

```python
import functools

import jax
import jax.numpy as jnp
from jax import lax
from jax.experimental import pallas as pl
from jax.experimental.pallas import tpu as pltpu
from jax.sharding import Mesh
from jax.sharding import PartitionSpec as P

LEAF = 64
LANES = 128

def spread(v, shape):
    return jnp.broadcast_to(v, shape)

def leaf_factor(block):
    groups = LEAF // 8
    full = (8, LANES)
    sub = lax.broadcasted_iota(jnp.int32, full, 0)
    x = [block[8 * i : 8 * i + 8] for i in range(groups)]
    done = []
    for kb in range(groups):
        cols = [
            [spread(x[i][:, 8 * kb + j : 8 * kb + j + 1], full) for i in range(kb, groups)]
            for j in range(8)
        ]
        pivots = jnp.ones(full, jnp.float32)
        for j in range(8):
            pivot = spread(cols[j][0][j : j + 1], full)
            pivots = jnp.where(sub == j, pivot, pivots)
            inverse = 1.0 / pivot
            tail = [spread(cols[jj][0][j : j + 1], full) * inverse for jj in range(j + 1, 8)]
            row = spread(x[kb][j : j + 1], full) * inverse
            for i in range(kb, groups):
                mult = cols[j][i - kb]
                if i == kb:
                    mult = jnp.where(sub > j, mult, 0.0)
                for jj in range(j + 1, 8):
                    cols[jj][i - kb] = cols[jj][i - kb] - mult * tail[jj - j - 1]
                x[i] = x[i] - mult * row
        done.append(x[kb] * (1.0 / jnp.sqrt(pivots)))
    return jnp.concatenate(done, axis=0)

def thirds(value):
    first = value.astype(jnp.bfloat16)
    rest = value - first.astype(jnp.float32)
    second = rest.astype(jnp.bfloat16)
    return first, second, (rest - second.astype(jnp.float32)).astype(jnp.bfloat16)


def six_left(value, axis):
    one, two, three = thirds(value)
    return jnp.concatenate([one, one, two, one, two, three], axis=axis)


def six_right(value):
    one, two, three = thirds(value)
    return jnp.concatenate([one, two, one, three, two, one], axis=0)


def factor_kernel(place_ref, mine_ref, other_ref, upper_ref, inverse_ref, work):
    size = work.shape[0]
    blocks = size // LEAF
    lane = lax.broadcasted_iota(jnp.int32, (LEAF, LANES), 1)
    sub = lax.broadcasted_iota(jnp.int32, (LEAF, LANES), 0)
    place = lax.broadcasted_iota(jnp.int32, (LEAF, size), 1)
    depth = lax.broadcasted_iota(jnp.int32, (LEAF, size), 0)
    y, core = place_ref[0], place_ref[1]
    for dy in range(4):
        owner = lax.rem(y + dy, 4)
        for ref, side in ((mine_ref, core), (other_ref, 1 - core)):
            for tile in range(ref.shape[1]):
                to = pl.multiple_of(128 * owner + 64 * side + 8 * (tile // 4), 8)
                lanes = pl.multiple_of(128 * lax.rem(owner + tile % 4, 4), 128)
                work[pl.ds(to, 8), pl.ds(lanes, 128)] = ref[dy, tile]
    late = None
    for b in range(blocks):
        lo, hi = LEAF * b, LEAF * b + LEAF
        tile = LANES * (b // 2)
        square = work[lo:hi, tile : tile + LANES]
        if b % 2:
            square = pltpu.roll(square, LEAF, 1)
        both = leaf_factor(
            jnp.where(lane < LEAF, square, jnp.where(lane == sub + LEAF, 1.0, 0.0))
        )
        other = pltpu.roll(both, LEAF, 1)
        inv = other[:, :LEAF]
        rows = jnp.dot(
            six_left(inv, 1), six_right(work[lo:hi, :]), preferred_element_type=jnp.float32
        )
        inv_wide = jnp.concatenate([both if b % 2 else other] * (size // LANES), axis=1)
        own = (place >= lo) & (place < hi)
        upper_ref[lo:hi, :] = jnp.where(place >= lo + depth, rows, 0.0)
        rows_inv = jnp.where(own, inv_wide, rows)
        inverse_ref[lo:hi, :] = jnp.where(place <= lo + depth, rows_inv, 0.0)
        if late is not None:
            late()
            late = None
        if b + 1 < blocks:
            mult = rows[:, hi - hi % LANES :]
            if hi % LANES:
                mult = mult[:, LEAF:]
            left, right = six_left(mult, 0), six_right(rows_inv)
            cut = min(hi + LEAF, size)

            def subtract(start, stop, lo=lo, hi=hi, left=left, right=right):
                step = lax.dot_general(
                    left[:, start - hi : stop - hi], right, (((0,), (0,)), ((), ())),
                    preferred_element_type=jnp.float32,
                )
                lanes = lax.broadcasted_iota(jnp.int32, (stop - start, size), 1)
                kept = jnp.where((lanes >= lo) & (lanes < hi), 0.0, work[start:stop, :])
                work[start:stop, :] = kept - step

            subtract(hi, cut)
            if cut < size:
                late = functools.partial(subtract, cut, size)


def factor(place, mine, other):
    size = 512
    return pl.pallas_call(
        factor_kernel,
        out_shape=[jax.ShapeDtypeStruct((size, size), jnp.float32)] * 2,
        in_specs=[
            pl.BlockSpec(memory_space=pltpu.SMEM),
            pl.BlockSpec(memory_space=pltpu.VMEM),
            pl.BlockSpec(memory_space=pltpu.VMEM),
        ],
        out_specs=[pl.BlockSpec(memory_space=pltpu.VMEM)] * 2,
        scratch_shapes=[pltpu.VMEM((size, size), jnp.float32)],
        compiler_params=pltpu.CompilerParams(vmem_limit_bytes=56 * 2**20),
        cost_estimate=pl.CostEstimate(
            flops=25 * 10**9, bytes_accessed=4 * 10**6, transcendentals=0
        ),
        name="factor",
    )(place, mine, other)


STEPS = 2


def halves(value):
    high = value.astype(jnp.bfloat16)
    return high, (value - high.astype(jnp.float32)).astype(jnp.bfloat16)


def product(a, b):
    return lax.dot_general(a, b, (((1,), (0,)), ((), ())), preferred_element_type=jnp.float32)


def dot3(both, high, right):
    rows = high.shape[0]
    right_high, right_low = halves(right)
    first = product(both, right_high)
    return first[:rows] + (first[rows:] + product(high, right_low))


def dot4(both, right):
    rows, cols = both.shape[0] // 2, right.shape[1]
    four = product(both, jnp.concatenate(halves(right), axis=1))
    return four[:rows, :cols] + (four[rows:, :cols] + four[:rows, cols:] + four[rows:, cols:])


def dot6(left, right):
    rows = left.shape[0]
    left, right = thirds(left), thirds(right)
    first = product(jnp.concatenate(left, axis=0), right[0])
    second = product(jnp.concatenate(left[:2], axis=0), right[1])
    small = first[2 * rows :] + (second[rows:] + product(left[0], right[2]))
    return first[:rows] + (first[rows : 2 * rows] + second[:rows] + small)


def chunk(k, length):
    return pl.ds(pl.multiple_of(k * length, 128), length)


def fetches(k, depth, trailing_ref, trailing_buf, block_refs, block_buf, sems, starts=None):
    part = chunk(k, depth)
    copies = [pltpu.make_async_copy(trailing_ref.at[part], trailing_buf.at[part], sems.at[k, 0])]
    at = 0
    for index, ref in enumerate(block_refs):
        rows = ref.shape[0]
        to = pl.ds(at if starts is None else pl.multiple_of(starts[index], 32), rows)
        copies.append(
            pltpu.make_async_copy(ref.at[:, part], block_buf.at[to, part], sems.at[k, index + 1])
        )
        at += rows
    return copies


def start_all(*places):
    for k in range(STEPS):
        for copy in fetches(k, *places):
            copy.start()


def wait_chunk(k, *places):
    for copy in fetches(k, *places):
        copy.wait()


def accumulate(places, rows, proj_ref, gram_ref):
    depth, _, trailing_buf, _, block_buf, _ = places
    own_at = rows if block_buf.shape[0] > rows else 0
    start_all(*places)
    proj_ref[...] = jnp.zeros_like(proj_ref)
    gram_ref[...] = jnp.zeros_like(gram_ref)

    @pl.loop(0, STEPS)
    def _(k):
        wait_chunk(k, *places)
        part = chunk(k, depth)
        high, low = halves(block_buf[:rows, part])
        both = jnp.concatenate([high, low], axis=0)
        proj_ref[...] += dot3(both, high, trailing_buf[part])
        gram_ref[...] += dot4(both, block_buf[own_at : own_at + 64, part].T)


def first_kernel(trailing_ref, *refs):
    *block_refs, proj_ref, gram_ref, trailing_buf, block_buf, sems = refs
    depth = trailing_ref.shape[0] // STEPS
    places = (depth, trailing_ref, trailing_buf, block_refs, block_buf, sems)
    accumulate(places, block_buf.shape[0], proj_ref, gram_ref)


def last_kernel(core_ref, trailing_ref, *refs):
    *block_refs, proj_early, gram_early, proj_out, gram_out = refs[:-5]
    trailing_buf, block_buf, sems, proj_ref, gram_ref = refs[-5:]
    depth = trailing_ref.shape[0] // STEPS
    places = (depth, trailing_ref, trailing_buf, block_refs, block_buf, sems)
    accumulate(places, proj_ref.shape[0], proj_ref, gram_ref)

    def ordered(early, late):
        return [early[0:128], early[128:256], late, early[256:384]]

    peers, per = proj_out.shape[0], proj_out.shape[1] // 2
    proj = jnp.concatenate(ordered(proj_early[...], proj_ref[...]), axis=0)
    for side in range(2):
        part = proj[:, 128 * side : 128 * side + 128]
        proj_out[:, per * side : per * side + per, :] = part.reshape(peers, per, 128)
    for place, pair in enumerate(ordered(gram_early[...], gram_ref[...])):
        tile = pair.T
        tile = jnp.where(core_ref[0] == 1, pltpu.roll(tile, 64, 1), tile)
        for group in range(tile.shape[0] // 8):
            gram_out[4 * group + place] = tile[8 * group : 8 * group + 8]


def whole_spec(shape):
    return pl.BlockSpec(memory_space=pltpu.VMEM)


def in_place():
    return pl.BlockSpec(memory_space=pl.ANY)


def float_shape(*shape):
    return jax.ShapeDtypeStruct(shape, jnp.float32)


def buffers(trailing, rows, blocks):
    return [
        pltpu.VMEM(trailing.shape, jnp.float32),
        pltpu.VMEM((rows, trailing.shape[0]), jnp.float32),
        pltpu.SemaphoreType.DMA((STEPS, 1 + len(blocks))),
    ]


def project_first(trailing, blocks):
    rows = sum(block.shape[0] for block in blocks)
    shapes = [(rows, trailing.shape[1]), (rows, 64)]
    return pl.pallas_call(
        first_kernel,
        out_shape=[float_shape(*shape) for shape in shapes],
        in_specs=[in_place()] * (1 + len(blocks)),
        out_specs=[whole_spec(shape) for shape in shapes],
        scratch_shapes=buffers(trailing, rows, blocks),
        compiler_params=pltpu.CompilerParams(vmem_limit_bytes=56 * 2**20),
        cost_estimate=pl.CostEstimate(
            flops=15 * 10**9, bytes_accessed=6 * 10**6, transcendentals=0
        ),
        name="project_first",
    )(trailing, *blocks)


def project_last(core, trailing, own, blocks, proj_early, gram_early, peers):
    rows = sum(block.shape[0] for block in blocks)
    size = rows + proj_early.shape[0]
    per = size // peers * (trailing.shape[1] // 128)
    shapes = [(peers, per, 128), (4 * own.shape[0] // 8, 8, 128)]
    return pl.pallas_call(
        last_kernel,
        out_shape=[float_shape(*shape) for shape in shapes],
        in_specs=[
            pl.BlockSpec(memory_space=pltpu.SMEM),
            *[in_place()] * (2 + len(blocks)),
            whole_spec(proj_early.shape),
            whole_spec(gram_early.shape),
        ],
        out_specs=[whole_spec(shape) for shape in shapes],
        scratch_shapes=[
            *buffers(trailing, rows + own.shape[0], [*blocks, own]),
            pltpu.VMEM((rows, trailing.shape[1]), jnp.float32),
            pltpu.VMEM((rows, own.shape[0]), jnp.float32),
        ],
        compiler_params=pltpu.CompilerParams(vmem_limit_bytes=56 * 2**20),
        cost_estimate=pl.CostEstimate(flops=10**9, bytes_accessed=6 * 10**6, transcendentals=0),
        name="project_last",
    )(core, trailing, *blocks, own, proj_early, gram_early)


def update_kernel(place_ref, proj_ref, inverse_ref, trailing_ref, *refs):
    *block_refs, coupling_ref, updated_ref = refs[:-6]
    trailing_buf, block_buf, sems, both_ref, hold_ref, out_sems = refs[-6:]
    depth = trailing_ref.shape[0] // STEPS
    cols = coupling_ref.shape[1]
    size = inverse_ref.shape[0]
    y, core = place_ref[0], place_ref[1]

    def column(dy, other):
        return 128 * lax.rem(y + dy, 4) + 64 * lax.rem(core + other, 2)

    starts = [column(0, 0), column(0, 1)]
    for dy in range(1, 4):
        for other in range(2):
            starts += [column(dy, other), column(dy, other) + 32]
    places = (depth, trailing_ref, trailing_buf, block_refs, block_buf, sems, starts)
    start_all(*places)
    peers, per = proj_ref.shape[0], proj_ref.shape[1] // 2
    sides = [proj_ref[:, per * s : per * s + per, :].reshape(size, 128) for s in range(2)]
    proj = jnp.concatenate(sides, axis=1)
    for dy in range(4):
        for other in range(2):
            slot = 64 * (2 * dy + other)
            to = pl.multiple_of(column(dy, other), 64)
            hold_ref[pl.ds(to, 64), :] = proj[slot : slot + 64]
    inverse = inverse_ref[...]
    coupling = dot6(inverse, hold_ref[...])
    coupling_ref[...] = coupling
    both_ref[:cols], both_ref[cols:] = halves(dot6(coupling.T, inverse))

    def send(k):
        part = chunk(k, depth)
        return pltpu.make_async_copy(trailing_buf.at[part], updated_ref.at[part], out_sems.at[k])

    @pl.loop(0, STEPS)
    def _(k):
        wait_chunk(k, *places)
        part = chunk(k, depth)
        change = dot3(both_ref[...], both_ref[:cols, :], block_buf[:, part])
        trailing_buf[part] = trailing_buf[part] - change.T
        send(k).start()

    for k in range(STEPS):
        send(k).wait()


def update(place, projected, inverse, trailing, blocks):
    size, cols = inverse.shape[0], trailing.shape[1]
    return pl.pallas_call(
        update_kernel,
        out_shape=[float_shape(size, cols), float_shape(*trailing.shape)],
        in_specs=[
            pl.BlockSpec(memory_space=pltpu.SMEM),
            whole_spec(projected.shape),
            whole_spec(inverse.shape),
            *[in_place()] * (1 + len(blocks)),
        ],
        out_specs=[whole_spec((size, cols)), in_place()],
        scratch_shapes=[
            *buffers(trailing, size, blocks),
            pltpu.VMEM((2 * cols, size), jnp.bfloat16),
            pltpu.VMEM((size, cols), jnp.float32),
            pltpu.SemaphoreType.DMA((STEPS,)),
        ],
        compiler_params=pltpu.CompilerParams(vmem_limit_bytes=56 * 2**20),
        cost_estimate=pl.CostEstimate(
            flops=3 * 10**9, bytes_accessed=13 * 10**6, transcendentals=0
        ),
        name="update",
    )(place, projected, inverse, trailing, *blocks)


def shift(value, axis, length, step):
    return lax.ppermute(value, axis, [(i, (i + step) % length) for i in range(length)])


def swap(value):
    return shift(value, "core", 2, 1)


def sum_over_rows(pieces):
    summed = jnp.sum(lax.all_to_all(pieces, ("z", "x"), 0, 0), axis=0)
    return lax.all_to_all(jnp.broadcast_to(summed, pieces.shape), ("z", "x"), 0, 0)


def on_device(panel_block, trailing):
    peers = lax.axis_size(("z", "x"))
    y, core = lax.axis_index("y"), lax.axis_index("core")
    own = panel_block.T
    low, high = own[:32], own[32:]
    own_other = swap(own)
    below_low, above_high = shift(low, "y", 4, 1), shift(high, "y", 4, -1)
    far = [shift(below_low, "y", 4, 1), shift(above_high, "y", 4, -1)]
    low, high, own_other = lax.optimization_barrier((low, high, own_other))
    below = [below_low, shift(high, "y", 4, 1)]
    above = [shift(low, "y", 4, -1), above_high]
    below_other, above_other = ([swap(v) for v in vs] for vs in (below, above))
    near = [own, own_other, *above, *above_other, *below, *below_other]
    early, far_now = lax.optimization_barrier((project_first(trailing, near), far))
    far_other = [swap(v) for v in far_now]
    proj, gram = project_last(core[None], trailing, own, [*far, *far_other], *early, peers)
    gram = sum_over_rows(gram)
    gram, proj = lax.optimization_barrier((gram, proj))
    grams = jnp.stack([gram, *(shift(gram, "y", 4, -dy) for dy in range(1, 4))])
    proj = sum_over_rows(proj)
    upper, inverse = factor(jnp.stack([y, core]), grams, swap(grams))
    blocks = [own, own_other, *above, *above_other, *far, *far_other, *below, *below_other]
    coupling, updated = update(jnp.stack([y, core]), proj, inverse, trailing, blocks)
    return (upper, coupling, updated)


def solution(mesh):
    physical = Mesh(mesh.devices.reshape(8, 4, 4, 2), ("z", "x", "y", "core"))
    row, col = ("z", "x"), ("y", "core")
    return jax.shard_map(
        on_device,
        mesh=physical,
        in_specs=(P(row, col), P(row, col)),
        out_specs=(P(), P(None, col), P(row, col)),
        check_vma=False,
    )
```

```python
import functools

import jax
import jax.numpy as jnp
from jax import lax
from jax.experimental import pallas as pl
from jax.experimental.pallas import tpu as pltpu
from jax.sharding import Mesh
from jax.sharding import PartitionSpec as P

LEAF = 64
LANES = 128

def spread(v, shape):
    return jnp.broadcast_to(v, shape)

def leaf_factor(block):
    groups = LEAF // 8
    full = (8, LANES)
    sub = lax.broadcasted_iota(jnp.int32, full, 0)
    x = [block[8 * i : 8 * i + 8] for i in range(groups)]
    done = []
    for kb in range(groups):
        cols = [
            [spread(x[i][:, 8 * kb + j : 8 * kb + j + 1], full) for i in range(kb, groups)]
            for j in range(8)
        ]
        pivots = jnp.ones(full, jnp.float32)
        for j in range(8):
            pivot = spread(cols[j][0][j : j + 1], full)
            pivots = jnp.where(sub == j, pivot, pivots)
            inverse = 1.0 / pivot
            tail = [spread(cols[jj][0][j : j + 1], full) * inverse for jj in range(j + 1, 8)]
            row = spread(x[kb][j : j + 1], full) * inverse
            for i in range(kb, groups):
                mult = cols[j][i - kb]
                if i == kb:
                    mult = jnp.where(sub > j, mult, 0.0)
                for jj in range(j + 1, 8):
                    cols[jj][i - kb] = cols[jj][i - kb] - mult * tail[jj - j - 1]
                x[i] = x[i] - mult * row
        done.append(x[kb] * (1.0 / jnp.sqrt(pivots)))
    return jnp.concatenate(done, axis=0)

def thirds(value):
    first = value.astype(jnp.bfloat16)
    rest = value - first.astype(jnp.float32)
    second = rest.astype(jnp.bfloat16)
    return first, second, (rest - second.astype(jnp.float32)).astype(jnp.bfloat16)


def six_left(value, axis):
    one, two, three = thirds(value)
    return jnp.concatenate([one, one, two, one, two, three], axis=axis)


def six_right(value):
    one, two, three = thirds(value)
    return jnp.concatenate([one, two, one, three, two, one], axis=0)


def factor_kernel(place_ref, mine_ref, other_ref, upper_ref, inverse_ref, work):
    size = work.shape[0]
    blocks = size // LEAF
    lane = lax.broadcasted_iota(jnp.int32, (LEAF, LANES), 1)
    sub = lax.broadcasted_iota(jnp.int32, (LEAF, LANES), 0)
    place = lax.broadcasted_iota(jnp.int32, (LEAF, size), 1)
    depth = lax.broadcasted_iota(jnp.int32, (LEAF, size), 0)
    y, core = place_ref[0], place_ref[1]
    for dy in range(4):
        owner = lax.rem(y + dy, 4)
        for ref, side in ((mine_ref, core), (other_ref, 1 - core)):
            for tile in range(ref.shape[1]):
                to = pl.multiple_of(128 * owner + 64 * side + 8 * (tile // 4), 8)
                lanes = pl.multiple_of(128 * lax.rem(owner + tile % 4, 4), 128)
                work[pl.ds(to, 8), pl.ds(lanes, 128)] = ref[dy, tile]
    late = None
    for b in range(blocks):
        lo, hi = LEAF * b, LEAF * b + LEAF
        tile = LANES * (b // 2)
        square = work[lo:hi, tile : tile + LANES]
        if b % 2:
            square = pltpu.roll(square, LEAF, 1)
        both = leaf_factor(
            jnp.where(lane < LEAF, square, jnp.where(lane == sub + LEAF, 1.0, 0.0))
        )
        other = pltpu.roll(both, LEAF, 1)
        inv = other[:, :LEAF]
        rows = jnp.dot(
            six_left(inv, 1), six_right(work[lo:hi, :]), preferred_element_type=jnp.float32
        )
        inv_wide = jnp.concatenate([both if b % 2 else other] * (size // LANES), axis=1)
        own = (place >= lo) & (place < hi)
        upper_ref[lo:hi, :] = jnp.where(place >= lo + depth, rows, 0.0)
        rows_inv = jnp.where(own, inv_wide, rows)
        inverse_ref[lo:hi, :] = jnp.where(place <= lo + depth, rows_inv, 0.0)
        if late is not None:
            late()
            late = None
        if b + 1 < blocks:
            mult = rows[:, hi - hi % LANES :]
            if hi % LANES:
                mult = mult[:, LEAF:]
            left, right = six_left(mult, 0), six_right(rows_inv)
            cut = min(hi + LEAF, size)

            def subtract(start, stop, lo=lo, hi=hi, left=left, right=right):
                step = lax.dot_general(
                    left[:, start - hi : stop - hi], right, (((0,), (0,)), ((), ())),
                    preferred_element_type=jnp.float32,
                )
                lanes = lax.broadcasted_iota(jnp.int32, (stop - start, size), 1)
                kept = jnp.where((lanes >= lo) & (lanes < hi), 0.0, work[start:stop, :])
                work[start:stop, :] = kept - step

            subtract(hi, cut)
            if cut < size:
                late = functools.partial(subtract, cut, size)


def factor(place, mine, other):
    size = 512
    return pl.pallas_call(
        factor_kernel,
        out_shape=[jax.ShapeDtypeStruct((size, size), jnp.float32)] * 2,
        in_specs=[
            pl.BlockSpec(memory_space=pltpu.SMEM),
            pl.BlockSpec(memory_space=pltpu.VMEM),
            pl.BlockSpec(memory_space=pltpu.VMEM),
        ],
        out_specs=[pl.BlockSpec(memory_space=pltpu.VMEM)] * 2,
        scratch_shapes=[pltpu.VMEM((size, size), jnp.float32)],
        compiler_params=pltpu.CompilerParams(vmem_limit_bytes=56 * 2**20),
        cost_estimate=pl.CostEstimate(
            flops=25 * 10**9, bytes_accessed=4 * 10**6, transcendentals=0
        ),
        name="factor",
    )(place, mine, other)


STEPS = 2


def halves(value):
    high = value.astype(jnp.bfloat16)
    return high, (value - high.astype(jnp.float32)).astype(jnp.bfloat16)


def product(a, b):
    return lax.dot_general(a, b, (((1,), (0,)), ((), ())), preferred_element_type=jnp.float32)


def dot3(both, high, right):
    rows = high.shape[0]
    right_high, right_low = halves(right)
    first = product(both, right_high)
    return first[:rows] + (first[rows:] + product(high, right_low))


def dot4(both, right):
    rows, cols = both.shape[0] // 2, right.shape[1]
    four = product(both, jnp.concatenate(halves(right), axis=1))
    return four[:rows, :cols] + (four[rows:, :cols] + four[:rows, cols:] + four[rows:, cols:])


def dot6(left, right):
    rows = left[0].shape[0]
    first = product(jnp.concatenate(left, axis=0), right[0])
    second = product(jnp.concatenate(left[:2], axis=0), right[1])
    small = first[2 * rows :] + (second[rows:] + product(left[0], right[2]))
    return first[:rows] + (first[rows : 2 * rows] + second[:rows] + small)


def chunk(k, length):
    return pl.ds(pl.multiple_of(k * length, 128), length)


def fetches(k, depth, trailing_ref, trailing_buf, block_refs, block_buf, sems, starts=None):
    part = chunk(k, depth)
    copies = [pltpu.make_async_copy(trailing_ref.at[part], trailing_buf.at[part], sems.at[k, 0])]
    at = 0
    for index, ref in enumerate(block_refs):
        rows = ref.shape[0]
        to = pl.ds(at if starts is None else pl.multiple_of(starts[index], 32), rows)
        copies.append(
            pltpu.make_async_copy(ref.at[:, part], block_buf.at[to, part], sems.at[k, index + 1])
        )
        at += rows
    return copies


def start_all(*places):
    for k in range(STEPS):
        for copy in fetches(k, *places):
            copy.start()


def wait_chunk(k, *places):
    for copy in fetches(k, *places):
        copy.wait()


def accumulate(places, rows, proj_ref, gram_ref):
    depth, _, trailing_buf, _, block_buf, _ = places
    own_at = rows if block_buf.shape[0] > rows else 0
    start_all(*places)
    proj_ref[...] = jnp.zeros_like(proj_ref)
    gram_ref[...] = jnp.zeros_like(gram_ref)

    @pl.loop(0, STEPS)
    def _(k):
        wait_chunk(k, *places)
        part = chunk(k, depth)
        high, low = halves(block_buf[:rows, part])
        both = jnp.concatenate([high, low], axis=0)
        proj_ref[...] += dot3(both, high, trailing_buf[part])
        gram_ref[...] += dot4(both, block_buf[own_at : own_at + 64, part].T)


def first_kernel(trailing_ref, *refs):
    *block_refs, proj_ref, gram_ref, trailing_buf, block_buf, sems = refs
    depth = trailing_ref.shape[0] // STEPS
    places = (depth, trailing_ref, trailing_buf, block_refs, block_buf, sems)
    accumulate(places, block_buf.shape[0], proj_ref, gram_ref)


def last_kernel(core_ref, trailing_ref, *refs):
    *block_refs, proj_early, gram_early, proj_out, gram_out = refs[:-5]
    trailing_buf, block_buf, sems, proj_ref, gram_ref = refs[-5:]
    depth = trailing_ref.shape[0] // STEPS
    places = (depth, trailing_ref, trailing_buf, block_refs, block_buf, sems)
    accumulate(places, proj_ref.shape[0], proj_ref, gram_ref)

    def ordered(early, late):
        return [early[0:128], early[128:256], late, early[256:384]]

    peers, per = proj_out.shape[0], proj_out.shape[1] // 2
    proj = jnp.concatenate(ordered(proj_early[...], proj_ref[...]), axis=0)
    for side in range(2):
        part = proj[:, 128 * side : 128 * side + 128]
        proj_out[:, per * side : per * side + per, :] = part.reshape(peers, per, 128)
    for place, pair in enumerate(ordered(gram_early[...], gram_ref[...])):
        tile = pair.T
        tile = jnp.where(core_ref[0] == 1, pltpu.roll(tile, 64, 1), tile)
        for group in range(tile.shape[0] // 8):
            gram_out[4 * group + place] = tile[8 * group : 8 * group + 8]


def whole_spec(shape):
    return pl.BlockSpec(memory_space=pltpu.VMEM)


def in_place():
    return pl.BlockSpec(memory_space=pl.ANY)


def float_shape(*shape):
    return jax.ShapeDtypeStruct(shape, jnp.float32)


def buffers(trailing, rows, blocks):
    return [
        pltpu.VMEM(trailing.shape, jnp.float32),
        pltpu.VMEM((rows, trailing.shape[0]), jnp.float32),
        pltpu.SemaphoreType.DMA((STEPS, 1 + len(blocks))),
    ]


def project_first(trailing, blocks):
    rows = sum(block.shape[0] for block in blocks)
    shapes = [(rows, trailing.shape[1]), (rows, 64)]
    return pl.pallas_call(
        first_kernel,
        out_shape=[float_shape(*shape) for shape in shapes],
        in_specs=[in_place()] * (1 + len(blocks)),
        out_specs=[whole_spec(shape) for shape in shapes],
        scratch_shapes=buffers(trailing, rows, blocks),
        compiler_params=pltpu.CompilerParams(vmem_limit_bytes=56 * 2**20),
        cost_estimate=pl.CostEstimate(
            flops=15 * 10**9, bytes_accessed=6 * 10**6, transcendentals=0
        ),
        name="project_first",
    )(trailing, *blocks)


def project_last(core, trailing, own, blocks, proj_early, gram_early, peers):
    rows = sum(block.shape[0] for block in blocks)
    size = rows + proj_early.shape[0]
    per = size // peers * (trailing.shape[1] // 128)
    shapes = [(peers, per, 128), (4 * own.shape[0] // 8, 8, 128)]
    return pl.pallas_call(
        last_kernel,
        out_shape=[float_shape(*shape) for shape in shapes],
        in_specs=[
            pl.BlockSpec(memory_space=pltpu.SMEM),
            *[in_place()] * (2 + len(blocks)),
            whole_spec(proj_early.shape),
            whole_spec(gram_early.shape),
        ],
        out_specs=[whole_spec(shape) for shape in shapes],
        scratch_shapes=[
            *buffers(trailing, rows + own.shape[0], [*blocks, own]),
            pltpu.VMEM((rows, trailing.shape[1]), jnp.float32),
            pltpu.VMEM((rows, own.shape[0]), jnp.float32),
        ],
        compiler_params=pltpu.CompilerParams(vmem_limit_bytes=56 * 2**20),
        cost_estimate=pl.CostEstimate(flops=10**9, bytes_accessed=6 * 10**6, transcendentals=0),
        name="project_last",
    )(core, trailing, *blocks, own, proj_early, gram_early)


def update_kernel(place_ref, proj_ref, inverse_ref, trailing_ref, *refs):
    *block_refs, coupling_ref, updated_ref = refs[:-6]
    trailing_buf, block_buf, sems, both_ref, hold_ref, out_sems = refs[-6:]
    depth = trailing_ref.shape[0] // STEPS
    cols = coupling_ref.shape[1]
    size = inverse_ref.shape[0]
    y, core = place_ref[0], place_ref[1]

    def column(dy, other):
        return 128 * lax.rem(y + dy, 4) + 64 * lax.rem(core + other, 2)

    starts = [column(0, 0), column(0, 1)]
    for dy in range(1, 4):
        for other in range(2):
            starts += [column(dy, other), column(dy, other) + 32]
    places = (depth, trailing_ref, trailing_buf, block_refs, block_buf, sems, starts)
    start_all(*places)
    peers, per = proj_ref.shape[0], proj_ref.shape[1] // 2
    sides = [proj_ref[:, per * s : per * s + per, :].reshape(size, 128) for s in range(2)]
    proj = jnp.concatenate(sides, axis=1)
    for dy in range(4):
        for other in range(2):
            slot = 64 * (2 * dy + other)
            to = pl.multiple_of(column(dy, other), 64)
            hold_ref[pl.ds(to, 64), :] = proj[slot : slot + 64]
    inverse = thirds(inverse_ref[...])
    coupling = dot6(inverse, thirds(hold_ref[...]))
    coupling_ref[...] = coupling
    both_ref[:cols], both_ref[cols:] = halves(dot6(thirds(coupling.T), inverse))

    def send(k):
        part = chunk(k, depth)
        return pltpu.make_async_copy(trailing_buf.at[part], updated_ref.at[part], out_sems.at[k])

    @pl.loop(0, STEPS)
    def _(k):
        wait_chunk(k, *places)
        part = chunk(k, depth)
        change = dot3(both_ref[...], both_ref[:cols, :], block_buf[:, part])
        trailing_buf[part] = trailing_buf[part] - change.T
        send(k).start()

    for k in range(STEPS):
        send(k).wait()


def update(place, projected, inverse, trailing, blocks):
    size, cols = inverse.shape[0], trailing.shape[1]
    return pl.pallas_call(
        update_kernel,
        out_shape=[float_shape(size, cols), float_shape(*trailing.shape)],
        in_specs=[
            pl.BlockSpec(memory_space=pltpu.SMEM),
            whole_spec(projected.shape),
            whole_spec(inverse.shape),
            *[in_place()] * (1 + len(blocks)),
        ],
        out_specs=[whole_spec((size, cols)), in_place()],
        scratch_shapes=[
            *buffers(trailing, size, blocks),
            pltpu.VMEM((2 * cols, size), jnp.bfloat16),
            pltpu.VMEM((size, cols), jnp.float32),
            pltpu.SemaphoreType.DMA((STEPS,)),
        ],
        compiler_params=pltpu.CompilerParams(vmem_limit_bytes=56 * 2**20),
        cost_estimate=pl.CostEstimate(
            flops=3 * 10**9, bytes_accessed=13 * 10**6, transcendentals=0
        ),
        name="update",
    )(place, projected, inverse, trailing, *blocks)


def shift(value, axis, length, step):
    return lax.ppermute(value, axis, [(i, (i + step) % length) for i in range(length)])


def swap(value):
    return shift(value, "core", 2, 1)


def sum_over_rows(pieces):
    summed = jnp.sum(lax.all_to_all(pieces, ("z", "x"), 0, 0), axis=0)
    return lax.all_to_all(jnp.broadcast_to(summed, pieces.shape), ("z", "x"), 0, 0)


def on_device(panel_block, trailing):
    peers = lax.axis_size(("z", "x"))
    y, core = lax.axis_index("y"), lax.axis_index("core")
    own = panel_block.T
    low, high = own[:32], own[32:]
    own_other = swap(own)
    below_low, above_high = shift(low, "y", 4, 1), shift(high, "y", 4, -1)
    far = [shift(below_low, "y", 4, 1), shift(above_high, "y", 4, -1)]
    low, high, own_other = lax.optimization_barrier((low, high, own_other))
    below = [below_low, shift(high, "y", 4, 1)]
    above = [shift(low, "y", 4, -1), above_high]
    below_other, above_other = ([swap(v) for v in vs] for vs in (below, above))
    near = [own, own_other, *above, *above_other, *below, *below_other]
    early, far_now = lax.optimization_barrier((project_first(trailing, near), far))
    far_other = [swap(v) for v in far_now]
    proj, gram = project_last(core[None], trailing, own, [*far, *far_other], *early, peers)
    gram = sum_over_rows(gram)
    gram, proj = lax.optimization_barrier((gram, proj))
    grams = jnp.stack([gram, *(shift(gram, "y", 4, -dy) for dy in range(1, 4))])
    proj = sum_over_rows(proj)
    upper, inverse = factor(jnp.stack([y, core]), grams, swap(grams))
    blocks = [own, own_other, *above, *above_other, *far, *far_other, *below, *below_other]
    coupling, updated = update(jnp.stack([y, core]), proj, inverse, trailing, blocks)
    return (upper, coupling, updated)


def solution(mesh):
    physical = Mesh(mesh.devices.reshape(8, 4, 4, 2), ("z", "x", "y", "core"))
    row, col = ("z", "x"), ("y", "core")
    return jax.shard_map(
        on_device,
        mesh=physical,
        in_specs=(P(row, col), P(row, col)),
        out_specs=(P(), P(None, col), P(row, col)),
        check_vma=False,
    )
```
